128 devices in a mesh: db: 4 (over z), seq: 32 (over x, y, core).
Axes of the slice: x: 4, y: 4, z: 4, core: 2. Of those that a mesh axis runs over, the one named last changes fastest.
Arguments:
- queries: bfloat16 [16384, 4096], P(('db', 'seq')), may hold values from -250 to 250
- encoded: bfloat16 [64, 128, 1024], P('db'), may hold values from -6 to 6
- key_weight: bfloat16 [1024, 4096], replicated, may hold values from -0.1875 to 0.1875
- value_weight: bfloat16 [1024, 4096], replicated, may hold values from -0.1875 to 0.1875
- nbr_shard: int32 [256, 2], P(('db', 'seq')), may hold values from 0 to 3, all different within a row; in each aligned block of 2 rows (0 to 1, 2 to 3, ...) at most 2 rows name the same one
- nbr_slot: int32 [256, 2], P(('db', 'seq')), may hold values from 0 to 15
Outputs:
- attended: bfloat16 [16384, 4096], P(('db', 'seq'))
The draws below stay inside these ranges and needn't reach their ends.
Inputs may be any that keep to these rules, and one draw needn't show every extreme that they name: `nbr_shard`: the 2 neighbours of one group lie in different shards; the neighbours of the groups of one device lie at most 2 in one shard, and exactly 2 in one shard for some device.
All inputs are finite; a program needn't handle non-finite values.
Results may differ from the reference program's by a relative error of at most 0.012.
The reference program's roundings to bfloat16 on the way count: a program that leaves them out, or rounds other values in their place, can miss the bound.
Values may be sent and summed in bfloat16 or wider, within the bound.
A program may use at most 128 MiB of HBM per device.

```python
import math
import jax
import jax.numpy as jnp
import numpy as np
from jax import lax

H = 32
HD = 128
DE = 1024
CL = 64
NB = 2
NT = 128
LENGTH = 2048
BLK_SH = 16
D = 4096
CH = 2
TOKENS = 16384
GROUPS = 256
ROWS = 64
CAP = 2
N_DB = 4


def draw_queries(key, part):
    key = jax.random.fold_in(key, 11)
    base = jax.random.normal(key, (TOKENS, D), jnp.float32)
    return jnp.clip(2.5 * base, -12.0, 12.0).astype(jnp.bfloat16)


def with_ends(entries, stream_key, low, largest):
    longest = entries.shape.index(max(entries.shape))
    spots = []
    for shift in (0, 1):
        where = [jax.random.randint(jax.random.fold_in(stream_key, axis), (), 0, length) for axis, length in enumerate(entries.shape)]
        where[longest] = (where[longest] + shift) % entries.shape[longest]
        spots.append(tuple(where))
    return entries.at[spots[0]].set(low).at[spots[1]].set(largest)


def level_of(rng, shape, cuts, smallest, high):
    factor_of, own = 1.0, jax.random.fold_in(rng, 6)
    for dim, blocks in cuts:
        draws = jnp.exp(jax.random.uniform(jax.random.fold_in(own, dim), (blocks,), jnp.float32, smallest / len(cuts), high / len(cuts)))
        factor_of = factor_of * jnp.repeat(draws, shape[dim] // blocks).reshape([-1 if axis == dim else 1 for axis in range(len(shape))])
    return factor_of


def deal_out(stream_key, own, number, rows, amount, top, limit, slope):
    ranking = jax.random.permutation(stream_key, amount)
    crowded, ordinary = load_shares(amount, rows * top, limit, slope, True), load_shares(amount, rows * top, limit, slope, False)
    places = jnp.arange(amount)

    def named(tallies, offset_by):
        used = int((tallies > 0).sum())
        fixed = max(1, used // 4)
        passed = fixed + (places - fixed + offset_by * (used - fixed)) % max(1, amount - fixed)
        return jnp.zeros((amount,), jnp.int32).at[ranking[jnp.where(places < fixed, places, passed)]].set(jnp.asarray(tallies, jnp.int32))

    tallies = jnp.where(number % 4 == 0, named(crowded, number // 4), named(ordinary, number - number // 4 - 1))
    mixed = jax.random.permutation(jax.random.fold_in(own, 3), amount)
    source_of, taker = mixed[0:amount // 2 * 2:2], mixed[1:amount // 2 * 2:2]
    slack = jnp.minimum(tallies[source_of] - 1, limit - tallies[taker]) // 2
    slack = jnp.where((source_of == ranking[0]) | (taker == ranking[0]) | (tallies[taker] == 0), 0, jnp.maximum(slack, 0))
    passed = jax.random.randint(jax.random.fold_in(own, 4), (amount // 2,), 0, 1 << 20) % (slack + 1)
    tallies = tallies.at[source_of].add(-passed).at[taker].add(passed)
    items = jnp.searchsorted(jnp.cumsum(tallies), jnp.arange(rows * top), side="right").astype(jnp.int32)
    table = items.reshape(top, rows).T
    table = table[jax.random.permutation(jax.random.fold_in(own, 1), rows)]
    offset_by = jax.random.randint(jax.random.fold_in(own, 2), (rows, 1), 0, top)
    return jnp.take_along_axis(table, (jnp.arange(top)[None, :] + offset_by) % top, axis=1)


def load_shares(number_of, total, most, lean, full):
    weights = [(1 << 20) // math.isqrt(rank ** lean) + 1 for rank in range(1, number_of + 1)]
    largest = most if full else min(most, max(-(-total // number_of), total * weights[0] // sum(weights)))
    least = 1 if total - largest >= number_of - 1 else 0
    counts, spare = [largest] + [least] * (number_of - 1), total - largest - least * (number_of - 1)
    while spare > 0:
        candidates = [i for i in range(1, number_of) if counts[i] < largest] or [i for i in range(1, number_of) if counts[i] < most]
        mass, remaining = sum([weights[i] for i in candidates]), spare
        for i in candidates:
            extra = min(most - counts[i], max(1, remaining * weights[i] // mass), spare)
            counts[i] = counts[i] + extra
            spare = spare - extra
    return np.array(counts)


def gaussian(stream_key, shape, scale, reach, shards=(), kind=jnp.bfloat16):
    array = scale * jax.random.normal(stream_key, shape, jnp.float32)
    if shards:
        array = array * level_of(stream_key, shape, shards, -0.22, 0.18)
    return jnp.clip(array, -reach, reach).astype(kind)


def setup_inputs(seed: int = 0) -> dict:
    splits = jax.random.split(jax.random.key(seed), 7)
    queries = draw_queries(jax.random.fold_in(splits[6], 71), 0)
    encoded = gaussian(splits[1], (ROWS, NT, DE), 1.0, 6.0, ((0, 4),))
    key_weight = gaussian(splits[2], (DE, D), DE ** -0.5, 0.1875)
    value_weight = gaussian(splits[3], (DE, D), DE ** -0.5, 0.1875)
    nbr_shard_keys = jax.random.split(jax.random.fold_in(splits[4], 1), GROUPS // CH)
    nbr_shard_turns = jax.random.permutation(jax.random.fold_in(splits[4], 3), GROUPS // CH)
    nbr_shard = jax.vmap(lambda own, number: deal_out(jax.random.fold_in(splits[4], 2), own, number, CH, N_DB, NB, CAP, 2))(nbr_shard_keys, nbr_shard_turns).reshape((GROUPS, NB))
    nbr_slot = with_ends(jax.random.randint(splits[5], (GROUPS, NB), 0, BLK_SH), jax.random.fold_in(splits[5], 1), 0, BLK_SH - 1).astype(jnp.int32)
    return dict(queries=queries, encoded=encoded, key_weight=key_weight, value_weight=value_weight, nbr_shard=nbr_shard, nbr_slot=nbr_slot)


def reference(queries, encoded, key_weight, value_weight, nbr_shard, nbr_slot):
    seq_count = TOKENS // LENGTH
    by_seq = queries.reshape(seq_count, LENGTH, D)
    tail = jnp.zeros((seq_count, CL - 1, D), queries.dtype)
    shifted = jnp.concatenate([by_seq[:, CL - 1:], tail], axis=1).reshape(GROUPS, CL, H, HD)
    flat_rows = (nbr_shard * BLK_SH + nbr_slot).astype(jnp.int32)

    def one_group(pair):
        block_q, picks = pair
        rows = jnp.take(encoded, picks, axis=0).reshape(NB * NT, DE)
        keys = jnp.dot(rows, key_weight, preferred_element_type=jnp.float32).astype(jnp.bfloat16)
        values = jnp.dot(rows, value_weight, preferred_element_type=jnp.float32).astype(jnp.bfloat16)
        keys = keys.reshape(NB * NT, H, HD)
        values = values.reshape(NB * NT, H, HD)
        scores = jnp.einsum('qhd,khd->hqk', block_q.astype(jnp.float32), keys.astype(jnp.float32)) / math.sqrt(HD)
        weights = jax.nn.softmax(scores, axis=-1).astype(jnp.bfloat16)
        mixed = jnp.einsum('hqk,khd->qhd', weights.astype(jnp.float32), values.astype(jnp.float32))
        return mixed.astype(jnp.bfloat16).reshape(CL, D)
    blocks = lax.map(one_group, (shifted, flat_rows)).reshape(seq_count, LENGTH, D)
    head = jnp.zeros((seq_count, CL - 1, D), blocks.dtype)
    attended = jnp.concatenate([head, blocks[:, :LENGTH - CL + 1]], axis=1)
    return attended.reshape(TOKENS, D)
```

```python
import functools
import math

import jax
import jax.numpy as jnp
from jax import lax
from jax.experimental import pallas as pl
from jax.experimental.pallas import tpu as pltpu
from jax.sharding import PartitionSpec as P

H = 32
HD = 128
DE = 1024
D = 4096
CL = 64
NB = 2
NT = 128
LENGTH = 2048
BLK_SH = 16
N_DB = 4
PER_SEQ = 16
CHUNKS = (64, 64)
TILE = 1024
MESH = pl.DeviceIdType.MESH


def kernel(
    queries, encoded, key_weight, value_weight, shard, slot, out,
    req, enc, wk, wv, q, q_next, q_rows, keys, values, picks, o_send, o_recv, o_own,
    *rest,
):
    n = len(CHUNKS)
    send = rest[:n]
    recv = rest[n : 2 * n]
    local_sem, req_send, req_recv, blk_send, blk_recv, q_sem, o_sem = rest[2 * n :]
    z = lax.axis_index("db")
    s = lax.axis_index("seq")
    base = (s // PER_SEQ) * PER_SEQ
    place = s % PER_SEQ
    ahead = (z, base + (place + 1) % PER_SEQ)
    behind = (z, base + (place + PER_SEQ - 1) % PER_SEQ)
    column = [((z + step) % N_DB, s) for step in (1, 2, 3)]

    load_enc = pltpu.make_async_copy(encoded, enc, local_sem.at[0])
    load_q = pltpu.make_async_copy(queries, q, local_sem.at[1])
    load_wk = pltpu.make_async_copy(key_weight, wk, local_sem.at[2])
    load_wv = pltpu.make_async_copy(value_weight, wv, local_sem.at[3])
    load_enc.start()
    load_q.start()
    load_wk.start()
    load_wv.start()

    for g in range(2):
        for j in range(NB):
            req[z, g * NB + j] = shard[g, j] * BLK_SH + slot[g, j]

    barrier = pltpu.get_barrier_semaphore()
    for partner in [*column, ahead, behind]:
        pl.semaphore_signal(barrier, inc=1, device_id=partner, device_id_type=MESH)
    pl.semaphore_wait(barrier, 5)

    asks = []
    for i, partner in enumerate(column):
        ask = pltpu.make_async_remote_copy(
            src_ref=req.at[z], dst_ref=req.at[z],
            send_sem=req_send.at[i], recv_sem=req_recv.at[i],
            device_id=partner, device_id_type=MESH,
        )
        ask.start()
        asks.append(ask)

    load_enc.wait()
    for ask in asks:
        ask.wait()

    def wanted(who, g, owner):
        first, second = req[who, g * NB], req[who, g * NB + 1]
        from_second = jnp.where(second // BLK_SH == owner, second % BLK_SH, 0)
        return jnp.where(first // BLK_SH == owner, first % BLK_SH, from_second)

    places = [[wanted((z + step) % N_DB, g, z) for g in range(2)] for step in range(N_DB)]
    blocks = []
    row = 0
    for c, rows in enumerate(CHUNKS):
        moves = []
        for i, partner in enumerate(column):
            for g in range(2):
                send[c][i, g] = enc[places[i + 1][g], row : row + rows, :]
            move = pltpu.make_async_remote_copy(
                src_ref=send[c].at[i], dst_ref=recv[c].at[z],
                send_sem=blk_send.at[c, i], recv_sem=blk_recv.at[c, i],
                device_id=partner, device_id_type=MESH,
            )
            move.start()
            moves.append(move)
        for g in range(2):
            recv[c][z, g] = enc[places[0][g], row : row + rows, :]
        blocks.append(moves)
        row += rows

    load_q.wait()
    give_q = pltpu.make_async_remote_copy(
        src_ref=q.at[pl.ds(0, CL)], dst_ref=q_next,
        send_sem=q_sem.at[0], recv_sem=q_sem.at[1],
        device_id=behind, device_id_type=MESH,
    )
    give_q.start()
    give_q.wait()

    def shift_q(i, carry):
        cols = pl.ds(pl.multiple_of(i * 512, 512), 512)
        both = jnp.concatenate([q[:, cols], q_next[:, cols]], axis=0).astype(jnp.float32)
        q_rows[:, cols] = pltpu.roll(both, 192 - (CL - 1), 0)[: 2 * CL].astype(jnp.bfloat16)
        return carry

    lax.fori_loop(0, D // 512, shift_q, 0)

    load_wk.wait()
    load_wv.wait()
    row = 0
    for c, rows in enumerate(CHUNKS):
        for move in blocks[c]:
            move.wait()
        for g in range(2):
            for j in range(NB):
                at = (g * NB + j) * rows
                picks[at : at + rows, :] = recv[c][shard[g, j], g]
        for weight, held in ((wk, keys), (wv, values)):

            def project(i, carry, weight=weight, held=held, row=row, rows=rows):
                cols = pl.ds(pl.multiple_of(i * TILE, TILE), TILE)
                done = jnp.dot(
                    picks[0 : 4 * rows, :], weight[:, cols], preferred_element_type=jnp.float32
                ).astype(jnp.bfloat16)
                for g in range(2):
                    held[g, NB * row : NB * (row + rows), cols] = done[g * NB * rows : (g + 1) * NB * rows]
                return carry

            lax.fori_loop(0, D // TILE, project, 0)
        row += rows

    def attend(g, into):
        def head(i, carry):
            for u in range(4):
                cols = pl.ds(pl.multiple_of((i * 4 + u) * HD, HD), HD)
                scores = lax.dot_general(
                    q_rows[g * CL : (g + 1) * CL, cols], keys[g, :, cols],
                    (((1,), (1,)), ((), ())), preferred_element_type=jnp.float32,
                ) * (1.0 / math.sqrt(HD))
                top = jnp.max(scores, axis=1, keepdims=True)
                raised = jnp.exp(scores - top)
                total = jnp.sum(raised, axis=1, keepdims=True)
                weights = (raised / total).astype(jnp.bfloat16)
                into[:, cols] = jnp.dot(
                    weights, values[g, :, cols], preferred_element_type=jnp.float32
                ).astype(jnp.bfloat16)
            return carry

        lax.fori_loop(0, H // 4, head, 0)

    attend(1, o_send)
    give_o = pltpu.make_async_remote_copy(
        src_ref=o_send, dst_ref=o_recv,
        send_sem=o_sem.at[0], recv_sem=o_sem.at[1],
        device_id=ahead, device_id_type=MESH,
    )
    give_o.start()
    attend(0, o_own)
    give_o.wait()

    opening = place == 0

    def finish(i, carry):
        cols = pl.ds(pl.multiple_of(i * 512, 512), 512)
        both = jnp.concatenate(
            [o_recv[:, cols], o_own[:, cols], o_send[0:16, cols]], axis=0
        ).astype(jnp.float32)
        moved = pltpu.roll(both, 2 * CL + 15, 0)[: 2 * CL]
        token = lax.broadcasted_iota(jnp.int32, (2 * CL, 512), 0)
        blank = jnp.logical_and(opening, token < CL - 1)
        out[:, cols] = jnp.where(blank, 0.0, moved).astype(jnp.bfloat16)
        return carry

    lax.fori_loop(0, D // 512, finish, 0)


def body(queries, encoded, key_weight, value_weight, nbr_shard, nbr_slot):
    n = len(CHUNKS)
    any_spec = pl.BlockSpec(memory_space=pl.ANY)
    smem = pl.BlockSpec(memory_space=pltpu.SMEM)
    bf16 = jnp.bfloat16
    return pl.pallas_call(
        kernel,
        out_shape=jax.ShapeDtypeStruct((2 * CL, D), bf16),
        in_specs=[any_spec] * 4 + [smem] * 2,
        out_specs=pl.BlockSpec(memory_space=pltpu.VMEM),
        scratch_shapes=[
            pltpu.SMEM((N_DB, 4), jnp.int32),
            pltpu.VMEM((BLK_SH, NT, DE), bf16),
            pltpu.VMEM((DE, D), bf16),
            pltpu.VMEM((DE, D), bf16),
            pltpu.VMEM((2 * CL, D), bf16),
            pltpu.VMEM((CL, D), bf16),
            pltpu.VMEM((2 * CL, D), bf16),
            pltpu.VMEM((2, NB * NT, D), bf16),
            pltpu.VMEM((2, NB * NT, D), bf16),
            pltpu.VMEM((4 * max(CHUNKS), DE), bf16),
            pltpu.VMEM((CL, D), bf16),
            pltpu.VMEM((CL, D), bf16),
            pltpu.VMEM((CL, D), bf16),
            *[pltpu.VMEM((3, 2, rows, DE), bf16) for rows in CHUNKS],
            *[pltpu.VMEM((N_DB, 2, rows, DE), bf16) for rows in CHUNKS],
            pltpu.SemaphoreType.DMA((4,)),
            pltpu.SemaphoreType.DMA((3,)),
            pltpu.SemaphoreType.DMA((3,)),
            pltpu.SemaphoreType.DMA((n, 3)),
            pltpu.SemaphoreType.DMA((n, 3)),
            pltpu.SemaphoreType.DMA((2,)),
            pltpu.SemaphoreType.DMA((2,)),
        ],
        compiler_params=pltpu.CompilerParams(
            collective_id=0, has_side_effects=True, vmem_limit_bytes=58 << 20
        ),
        name="retro",
    )(queries, encoded, key_weight, value_weight, nbr_shard, nbr_slot)


def solution(mesh):
    placed = (
        P(("db", "seq"), None),
        P("db", None, None),
        P(),
        P(),
        P(("db", "seq"), None),
        P(("db", "seq"), None),
    )
    return jax.shard_map(
        body, mesh=mesh, in_specs=placed, out_specs=P(("db", "seq"), None), check_vma=False
    )
```

```python
import functools
import math

import jax
import jax.numpy as jnp
from jax import lax
from jax.experimental import pallas as pl
from jax.experimental.pallas import tpu as pltpu
from jax.sharding import PartitionSpec as P

H = 32
HD = 128
DE = 1024
D = 4096
CL = 64
NB = 2
NT = 128
LENGTH = 2048
BLK_SH = 16
N_DB = 4
PER_SEQ = 16
CHUNKS = (32, 32, 32, 32)
TILE = 2048
HEADS = 16
SCALE = math.log2(math.e) / math.sqrt(HD)
MESH = pl.DeviceIdType.MESH


def kernel(
    queries, encoded, key_weight, value_weight, shard, slot, out,
    mine, req, enc, wk, wv, q, q_prev, q_rows, keys, values, picks, row_send, row_recv,
    *rest,
):
    n = len(CHUNKS)
    send = rest[:n]
    recv = rest[n : 2 * n]
    local_sem, req_send, req_recv, blk_send, blk_recv, q_sem, row_sem = rest[2 * n :]
    z = lax.axis_index("db")
    s = lax.axis_index("seq")
    base = (s // PER_SEQ) * PER_SEQ
    place = s % PER_SEQ
    ahead = base + (place + 1) % PER_SEQ
    behind = base + (place + PER_SEQ - 1) % PER_SEQ

    load_enc = pltpu.make_async_copy(encoded, enc, local_sem.at[0])
    load_q = pltpu.make_async_copy(queries, q, local_sem.at[1])
    load_wk = pltpu.make_async_copy(key_weight, wk, local_sem.at[2])
    load_wv = pltpu.make_async_copy(value_weight, wv, local_sem.at[3])
    load_enc.start()
    load_q.start()
    load_wk.start()
    load_wv.start()

    for g in range(2):
        for j in range(NB):
            wanted = shard[g, j] * BLK_SH + slot[g, j]
            mine[1 - g, j] = wanted
            if g == 0:
                req[z, 1, j] = wanted

    barrier = pltpu.get_barrier_semaphore()

    def tell(where):
        pl.semaphore_signal(barrier, inc=1, device_id=where, device_id_type=MESH)

    tell((z, ahead))
    for step in range(N_DB):
        tell(((z + step) % N_DB, behind))
        if step:
            tell(((z + step) % N_DB, s))
    pl.semaphore_wait(barrier, 2 * N_DB)

    asks = []
    for step in range(N_DB):
        for g in range(2):
            if g == 1 and step == 0:
                continue
            ask = pltpu.make_async_remote_copy(
                src_ref=mine.at[g], dst_ref=req.at[z, g],
                send_sem=req_send.at[g, step], recv_sem=req_recv.at[g, step],
                device_id=((z + step) % N_DB, ahead if g == 0 else s), device_id_type=MESH,
            )
            ask.start()
            asks.append(ask)
    give_q = pltpu.make_async_remote_copy(
        src_ref=queries.at[pl.ds(2 * CL - 16, 16)], dst_ref=q_prev,
        send_sem=q_sem.at[0], recv_sem=q_sem.at[1],
        device_id=(z, ahead), device_id_type=MESH,
    )
    give_q.start()

    load_enc.wait()
    for ask in asks:
        ask.wait()

    def place_in(who, g):
        first, second = req[who, g, 0], req[who, g, 1]
        from_second = jnp.where(second // BLK_SH == z, second % BLK_SH, 0)
        return jnp.where(first // BLK_SH == z, first % BLK_SH, from_second)

    places = [[place_in((z + step) % N_DB, g) for g in range(2)] for step in range(N_DB)]
    owners = [[req[z, g, j] // BLK_SH for j in range(NB)] for g in range(2)]
    blocks = []
    row = 0
    for c, rows in enumerate(CHUNKS):
        moves = []
        for i in range(3):
            for g in range(2):
                send[c][i, g] = enc[places[i + 1][g], row : row + rows, :]
            move = pltpu.make_async_remote_copy(
                src_ref=send[c].at[i], dst_ref=recv[c].at[z],
                send_sem=blk_send.at[c, i], recv_sem=blk_recv.at[c, i],
                device_id=((z + i + 1) % N_DB, s), device_id_type=MESH,
            )
            move.start()
            moves.append(move)
        for g in range(2):
            recv[c][z, g] = enc[places[0][g], row : row + rows, :]
        blocks.append(moves)
        row += rows

    load_q.wait()
    give_q.wait()

    def shift_q(i, carry):
        cols = pl.ds(pl.multiple_of(i * 512, 512), 512)
        both = jnp.concatenate([q_prev[:, cols], q[:, cols]], axis=0).astype(jnp.float32)
        q_rows[:, cols] = pltpu.roll(both, 2 * CL + 1, 0)[: 2 * CL].astype(jnp.bfloat16)
        return carry

    lax.fori_loop(0, D // 512, shift_q, 0)

    load_wk.wait()
    load_wv.wait()
    row = 0
    for c, rows in enumerate(CHUNKS):
        for move in blocks[c]:
            move.wait()
        for g in range(2):
            for j in range(NB):
                at = (g * NB + j) * rows
                picks[at : at + rows, :] = recv[c][owners[g][j], g]
        for weight, held in ((wk, keys), (wv, values)):

            def project(i, carry, weight=weight, held=held, row=row, rows=rows):
                cols = pl.ds(pl.multiple_of(i * TILE, TILE), TILE)
                done = jnp.dot(
                    picks[0 : 4 * rows, :], weight[:, cols], preferred_element_type=jnp.float32
                ).astype(jnp.bfloat16)
                for g in range(2):
                    held[g, NB * row : NB * (row + rows), cols] = done[g * NB * rows : (g + 1) * NB * rows]
                return carry

            lax.fori_loop(0, D // TILE, project, 0)
        row += rows

    def attend(g, half):
        heads = [pl.ds((half * HEADS + u) * HD, HD) for u in range(HEADS)]
        scores = [
            lax.dot_general(
                q_rows[g * CL : (g + 1) * CL, cols], keys[g, :, cols],
                (((1,), (1,)), ((), ())), preferred_element_type=jnp.float32,
            )
            for cols in heads
        ]
        tops = [jnp.max(score, axis=1, keepdims=True) for score in scores]
        raised = [jnp.exp2((score - top) * SCALE) for score, top in zip(scores, tops)]
        totals = [jnp.sum(each, axis=1, keepdims=True) for each in raised]
        weights = [
            (each * (1.0 / total)).astype(jnp.bfloat16) for each, total in zip(raised, totals)
        ]
        mixed = [
            jnp.dot(weight, values[g, :, cols], preferred_element_type=jnp.float32)
            for weight, cols in zip(weights, heads)
        ]
        return list(zip(heads, mixed))

    for half in range(H // HEADS):
        done = attend(0, half)
        for cols, each in done:
            moved = jnp.where(place == 0, 0.0, pltpu.roll(each, CL - 1, 0))
            out[0:CL, cols] = moved.astype(jnp.bfloat16)
        row_send[half * HEADS : (half + 1) * HEADS, :] = jnp.concatenate(
            [each[0:1] for _, each in done], axis=0
        ).astype(jnp.bfloat16)
    give_row = pltpu.make_async_remote_copy(
        src_ref=row_send, dst_ref=row_recv,
        send_sem=row_sem.at[0], recv_sem=row_sem.at[1],
        device_id=(z, behind), device_id_type=MESH,
    )
    give_row.start()
    for half in range(H // HEADS):
        for cols, each in attend(1, half):
            out[CL : 2 * CL, cols] = pltpu.roll(each, CL - 1, 0).astype(jnp.bfloat16)
            out[CL - 1 : CL, cols] = each[0:1].astype(jnp.bfloat16)
    give_row.wait()
    last = row_recv[...]
    for h in range(H):
        out[2 * CL - 1 : 2 * CL, h * HD : (h + 1) * HD] = last[h : h + 1]


def body(queries, encoded, key_weight, value_weight, nbr_shard, nbr_slot):
    n = len(CHUNKS)
    any_spec = pl.BlockSpec(memory_space=pl.ANY)
    smem = pl.BlockSpec(memory_space=pltpu.SMEM)
    bf16 = jnp.bfloat16
    return pl.pallas_call(
        kernel,
        out_shape=jax.ShapeDtypeStruct((2 * CL, D), bf16),
        in_specs=[any_spec] * 4 + [smem] * 2,
        out_specs=pl.BlockSpec(memory_space=pltpu.VMEM),
        scratch_shapes=[
            pltpu.SMEM((2, NB), jnp.int32),
            pltpu.SMEM((N_DB, 2, NB), jnp.int32),
            pltpu.VMEM((BLK_SH, NT, DE), bf16),
            pltpu.VMEM((DE, D), bf16),
            pltpu.VMEM((DE, D), bf16),
            pltpu.VMEM((2 * CL, D), bf16),
            pltpu.VMEM((16, D), bf16),
            pltpu.VMEM((2 * CL, D), bf16),
            pltpu.VMEM((2, NB * NT, D), bf16),
            pltpu.VMEM((2, NB * NT, D), bf16),
            pltpu.VMEM((4 * max(CHUNKS), DE), bf16),
            pltpu.VMEM((H, HD), bf16),
            pltpu.VMEM((H, HD), bf16),
            *[pltpu.VMEM((3, 2, rows, DE), bf16) for rows in CHUNKS],
            *[pltpu.VMEM((N_DB, 2, rows, DE), bf16) for rows in CHUNKS],
            pltpu.SemaphoreType.DMA((4,)),
            pltpu.SemaphoreType.DMA((2, N_DB)),
            pltpu.SemaphoreType.DMA((2, N_DB)),
            pltpu.SemaphoreType.DMA((n, 3)),
            pltpu.SemaphoreType.DMA((n, 3)),
            pltpu.SemaphoreType.DMA((2,)),
            pltpu.SemaphoreType.DMA((2,)),
        ],
        compiler_params=pltpu.CompilerParams(
            collective_id=0, has_side_effects=True, vmem_limit_bytes=58 << 20
        ),
        name="retro",
    )(queries, encoded, key_weight, value_weight, nbr_shard, nbr_slot)


def solution(mesh):
    placed = (
        P(("db", "seq"), None),
        P("db", None, None),
        P(),
        P(),
        P(("db", "seq"), None),
        P(("db", "seq"), None),
    )
    return jax.shard_map(
        body, mesh=mesh, in_specs=placed, out_specs=P(("db", "seq"), None), check_vma=False
    )
```

```python
import functools
import math

import jax
import jax.numpy as jnp
from jax import lax
from jax.experimental import pallas as pl
from jax.experimental.pallas import tpu as pltpu
from jax.sharding import PartitionSpec as P

H = 32
HD = 128
DE = 1024
D = 4096
CL = 64
NB = 2
NT = 128
LENGTH = 2048
BLK_SH = 16
N_DB = 4
SIDE = 4
PER_SEQ = 16
CHUNKS = (32, 32, 32, 32)
TILE = 2048
HEADS = 16
SCALE = math.log2(math.e) / math.sqrt(HD)
MESH = pl.DeviceIdType.MESH


def kernel(
    queries, encoded, key_weight, value_weight, shard, slot, out,
    mine, req, enc, wk, wv, q, q_prev, q_rows, keys, values, picks, row_send, row_recv,
    *rest,
):
    n = len(CHUNKS)
    send = rest[:n]
    recv = rest[n : 2 * n]
    far = rest[2 * n : 3 * n]
    (
        local_sem, req_send, req_recv, blk_send, blk_recv, far_send, far_recv, q_sem, row_sem,
    ) = rest[3 * n :]
    z = lax.axis_index("db")
    s = lax.axis_index("seq")
    base = (s // PER_SEQ) * PER_SEQ
    place = s % PER_SEQ
    ahead = base + (place + 1) % PER_SEQ
    behind = base + (place + PER_SEQ - 1) % PER_SEQ
    block, core = s // 2, s % 2
    u = jnp.where(core == 0, block // SIDE, block % SIDE)
    v = jnp.where(core == 0, block % SIDE, block // SIDE)
    spot = u * SIDE + v

    def chip(u_of, v_of):
        x = jnp.where(core == 0, u_of, v_of)
        y = jnp.where(core == 0, v_of, u_of)
        return (z, (x * SIDE + y) * 2 + core)

    opposite = ((z + 2) % N_DB, s)
    other_core = (z, block * 2 + 1 - core)
    along_v = [chip(u, (v + step) % SIDE) for step in (1, 3, 2)]
    along_u = [chip((u + step) % SIDE, v) for step in (1, 3, 2)]
    near = [((z + step) % N_DB, s) for step in (1, 3)]

    load_enc = pltpu.make_async_copy(encoded, enc, local_sem.at[0])
    load_q = pltpu.make_async_copy(queries, q, local_sem.at[1])
    load_wk = pltpu.make_async_copy(key_weight, wk, local_sem.at[2])
    load_wv = pltpu.make_async_copy(value_weight, wv, local_sem.at[3])
    load_enc.start()
    load_q.start()
    load_wk.start()
    load_wv.start()

    for g in range(2):
        for j in range(NB):
            wanted = shard[g, j] * BLK_SH + slot[g, j]
            mine[1 - g, j] = wanted
            if g == 0:
                req[z, 1, j] = wanted

    barrier = pltpu.get_barrier_semaphore()

    def tell(where):
        pl.semaphore_signal(barrier, inc=1, device_id=where, device_id_type=MESH)

    tell((z, ahead))
    for step in (0, 1, 3):
        tell(((z + step) % N_DB, behind))
    for partner in [*near, opposite, *along_v, *along_u, other_core]:
        tell(partner)
    pl.semaphore_wait(barrier, 14)

    brings = []
    row = 0
    for c, rows in enumerate(CHUNKS):
        half = rows // 2
        bring = pltpu.make_async_remote_copy(
            src_ref=encoded.at[block, pl.ds(row + core * half, half)], dst_ref=far[c].at[core, spot],
            send_sem=far_send.at[c, 0], recv_sem=far_recv.at[c, 0],
            device_id=opposite, device_id_type=MESH,
        )
        bring.start()
        brings.append(bring)
        row += rows

    asks = []
    for i, step in enumerate((0, 1, 3)):
        for g in range(2):
            if g == 1 and step == 0:
                continue
            ask = pltpu.make_async_remote_copy(
                src_ref=mine.at[g], dst_ref=req.at[z, g],
                send_sem=req_send.at[g, i], recv_sem=req_recv.at[g, i],
                device_id=((z + step) % N_DB, ahead if g == 0 else s), device_id_type=MESH,
            )
            ask.start()
            asks.append(ask)
    give_q = pltpu.make_async_remote_copy(
        src_ref=queries.at[pl.ds(2 * CL - 16, 16)], dst_ref=q_prev,
        send_sem=q_sem.at[0], recv_sem=q_sem.at[1],
        device_id=(z, ahead), device_id_type=MESH,
    )
    give_q.start()

    def spread(c, first, partners, source):
        moves = []
        for i, partner in enumerate(partners):
            move = pltpu.make_async_remote_copy(
                src_ref=source, dst_ref=source,
                send_sem=far_send.at[c, first + i], recv_sem=far_recv.at[c, first + i],
                device_id=partner, device_id_type=MESH,
            )
            move.start()
            moves.append(move)
        return moves

    def pieces(c):
        brings[c].wait()
        return spread(c, 1, along_v, far[c].at[core, spot])

    def bundles(c, moves):
        for move in moves:
            move.wait()
        return spread(c, 4, along_u, far[c].at[core, pl.ds(u * SIDE, SIDE)])

    def share(c, moves):
        for move in moves:
            move.wait()
        return spread(c, 7, [other_core], far[c].at[core])

    ones = [pieces(0)]
    load_enc.wait()
    for ask in asks:
        ask.wait()

    def place_in(who, g, owner):
        first, second = req[who, g, 0], req[who, g, 1]
        from_second = jnp.where(second // BLK_SH == owner, second % BLK_SH, 0)
        return jnp.where(first // BLK_SH == owner, first % BLK_SH, from_second)

    places = [[place_in((z + step) % N_DB, g, z) for g in range(2)] for step in (0, 1, 3)]
    far_places = [place_in(z, g, (z + 2) % N_DB) for g in range(2)]
    owners = [[req[z, g, j] // BLK_SH for j in range(NB)] for g in range(2)]
    blocks = []
    row = 0
    for c, rows in enumerate(CHUNKS):
        moves = []
        for i, partner in enumerate(near):
            for g in range(2):
                send[c][i, g] = enc[places[i + 1][g], row : row + rows, :]
            move = pltpu.make_async_remote_copy(
                src_ref=send[c].at[i], dst_ref=recv[c].at[z],
                send_sem=blk_send.at[c, i], recv_sem=blk_recv.at[c, i],
                device_id=partner, device_id_type=MESH,
            )
            move.start()
            moves.append(move)
        for g in range(2):
            recv[c][z, g] = enc[places[0][g], row : row + rows, :]
        blocks.append(moves)
        row += rows

    twos = []
    for c in range(1, n):
        ones.append(pieces(c))
        twos.append(bundles(c - 1, ones[c - 1]))
    twos.append(bundles(n - 1, ones[n - 1]))

    load_q.wait()
    give_q.wait()

    def shift_q(i, carry):
        cols = pl.ds(pl.multiple_of(i * 512, 512), 512)
        both = jnp.concatenate([q_prev[:, cols], q[:, cols]], axis=0).astype(jnp.float32)
        q_rows[:, cols] = pltpu.roll(both, 2 * CL + 1, 0)[: 2 * CL].astype(jnp.bfloat16)
        return carry

    lax.fori_loop(0, D // 512, shift_q, 0)

    shares = [share(0, twos[0])]
    load_wk.wait()
    load_wv.wait()
    row = 0
    for c, rows in enumerate(CHUNKS):
        half = rows // 2
        for move in [*blocks[c], *shares[c]]:
            move.wait()
        for g in range(2):
            at = far_places[g]
            recv[c][(z + 2) % N_DB, g, 0:half] = far[c][0, at]
            recv[c][(z + 2) % N_DB, g, half:rows] = far[c][1, at % SIDE * SIDE + at // SIDE]
        for g in range(2):
            for j in range(NB):
                at = (g * NB + j) * rows
                picks[at : at + rows, :] = recv[c][owners[g][j], g]
        for weight, held in ((wk, keys), (wv, values)):

            def project(i, carry, weight=weight, held=held, row=row, rows=rows):
                cols = pl.ds(pl.multiple_of(i * TILE, TILE), TILE)
                done = jnp.dot(
                    picks[0 : 4 * rows, :], weight[:, cols], preferred_element_type=jnp.float32
                ).astype(jnp.bfloat16)
                for g in range(2):
                    held[g, NB * row : NB * (row + rows), cols] = done[g * NB * rows : (g + 1) * NB * rows]
                return carry

            lax.fori_loop(0, D // TILE, project, 0)
            if weight is wk and c + 1 < n:
                shares.append(share(c + 1, twos[c + 1]))
        row += rows

    def attend(g, half):
        heads = [pl.ds((half * HEADS + u) * HD, HD) for u in range(HEADS)]
        scores = [
            lax.dot_general(
                q_rows[g * CL : (g + 1) * CL, cols], keys[g, :, cols],
                (((1,), (1,)), ((), ())), preferred_element_type=jnp.float32,
            )
            for cols in heads
        ]
        tops = [jnp.max(score, axis=1, keepdims=True) for score in scores]
        raised = [jnp.exp2((score - top) * SCALE) for score, top in zip(scores, tops)]
        totals = [jnp.sum(each, axis=1, keepdims=True) for each in raised]
        weights = [
            (each * (1.0 / total)).astype(jnp.bfloat16) for each, total in zip(raised, totals)
        ]
        mixed = [
            jnp.dot(weight, values[g, :, cols], preferred_element_type=jnp.float32)
            for weight, cols in zip(weights, heads)
        ]
        return list(zip(heads, mixed))

    for half in range(H // HEADS):
        done = attend(0, half)
        for cols, each in done:
            moved = jnp.where(place == 0, 0.0, pltpu.roll(each, CL - 1, 0))
            out[0:CL, cols] = moved.astype(jnp.bfloat16)
        row_send[half * HEADS : (half + 1) * HEADS, :] = jnp.concatenate(
            [each[0:1] for _, each in done], axis=0
        ).astype(jnp.bfloat16)
    give_row = pltpu.make_async_remote_copy(
        src_ref=row_send, dst_ref=row_recv,
        send_sem=row_sem.at[0], recv_sem=row_sem.at[1],
        device_id=(z, behind), device_id_type=MESH,
    )
    give_row.start()
    for half in range(H // HEADS):
        for cols, each in attend(1, half):
            out[CL : 2 * CL, cols] = pltpu.roll(each, CL - 1, 0).astype(jnp.bfloat16)
            out[CL - 1 : CL, cols] = each[0:1].astype(jnp.bfloat16)
    give_row.wait()
    last = row_recv[...]
    for h in range(H):
        out[2 * CL - 1 : 2 * CL, h * HD : (h + 1) * HD] = last[h : h + 1]


def body(queries, encoded, key_weight, value_weight, nbr_shard, nbr_slot):
    n = len(CHUNKS)
    any_spec = pl.BlockSpec(memory_space=pl.ANY)
    smem = pl.BlockSpec(memory_space=pltpu.SMEM)
    bf16 = jnp.bfloat16
    return pl.pallas_call(
        kernel,
        out_shape=jax.ShapeDtypeStruct((2 * CL, D), bf16),
        in_specs=[any_spec] * 4 + [smem] * 2,
        out_specs=pl.BlockSpec(memory_space=pltpu.VMEM),
        scratch_shapes=[
            pltpu.SMEM((2, NB), jnp.int32),
            pltpu.SMEM((N_DB, 2, NB), jnp.int32),
            pltpu.VMEM((BLK_SH, NT, DE), bf16),
            pltpu.VMEM((DE, D), bf16),
            pltpu.VMEM((DE, D), bf16),
            pltpu.VMEM((2 * CL, D), bf16),
            pltpu.VMEM((16, D), bf16),
            pltpu.VMEM((2 * CL, D), bf16),
            pltpu.VMEM((2, NB * NT, D), bf16),
            pltpu.VMEM((2, NB * NT, D), bf16),
            pltpu.VMEM((4 * max(CHUNKS), DE), bf16),
            pltpu.VMEM((H, HD), bf16),
            pltpu.VMEM((H, HD), bf16),
            *[pltpu.VMEM((2, 2, rows, DE), bf16) for rows in CHUNKS],
            *[pltpu.VMEM((N_DB, 2, rows, DE), bf16) for rows in CHUNKS],
            *[pltpu.VMEM((2, BLK_SH, rows // 2, DE), bf16) for rows in CHUNKS],
            pltpu.SemaphoreType.DMA((4,)),
            pltpu.SemaphoreType.DMA((2, 3)),
            pltpu.SemaphoreType.DMA((2, 3)),
            pltpu.SemaphoreType.DMA((n, 2)),
            pltpu.SemaphoreType.DMA((n, 2)),
            pltpu.SemaphoreType.DMA((n, 8)),
            pltpu.SemaphoreType.DMA((n, 8)),
            pltpu.SemaphoreType.DMA((2,)),
            pltpu.SemaphoreType.DMA((2,)),
        ],
        compiler_params=pltpu.CompilerParams(
            collective_id=0, has_side_effects=True, vmem_limit_bytes=58 << 20
        ),
        name="retro",
    )(queries, encoded, key_weight, value_weight, nbr_shard, nbr_slot)


def solution(mesh):
    placed = (
        P(("db", "seq"), None),
        P("db", None, None),
        P(),
        P(),
        P(("db", "seq"), None),
        P(("db", "seq"), None),
    )
    return jax.shard_map(
        body, mesh=mesh, in_specs=placed, out_specs=P(("db", "seq"), None), check_vma=False
    )
```

```python
import functools
import math

import jax
import jax.numpy as jnp
from jax import lax
from jax.experimental import pallas as pl
from jax.experimental.pallas import tpu as pltpu
from jax.sharding import PartitionSpec as P

H = 32
HD = 128
DE = 1024
D = 4096
CL = 64
NB = 2
NT = 128
LENGTH = 2048
BLK_SH = 16
N_DB = 4
SIDE = 4
PER_SEQ = 16
CHUNKS = (32, 32, 32, 32)
DIRECT = 1
PLAN = {(0, False): (1,), (1, False): (2,), (2, False): (3,)}
TILE = 4096
HEADS = 16
SCALE = math.log2(math.e) / math.sqrt(HD)
MESH = pl.DeviceIdType.MESH


def kernel(
    queries, encoded, key_weight, value_weight, shard, slot, out,
    mine, req, enc, wk, wv, q, q_prev, q_rows, keys, values, picks, row_send, row_recv,
    *rest,
):
    n = len(CHUNKS)
    send = rest[:n]
    recv = rest[n : 2 * n]
    far = rest[2 * n : 3 * n]
    (
        local_sem, req_send, req_recv, blk_send, blk_recv, far_send, far_recv, q_sem, row_sem,
    ) = rest[3 * n :]
    z = lax.axis_index("db")
    s = lax.axis_index("seq")
    base = (s // PER_SEQ) * PER_SEQ
    place = s % PER_SEQ
    ahead = base + (place + 1) % PER_SEQ
    behind = base + (place + PER_SEQ - 1) % PER_SEQ
    block, core = s // 2, s % 2
    u = jnp.where(core == 0, block // SIDE, block % SIDE)
    v = jnp.where(core == 0, block % SIDE, block // SIDE)
    spot = u * SIDE + v

    def chip(u_of, v_of):
        x = jnp.where(core == 0, u_of, v_of)
        y = jnp.where(core == 0, v_of, u_of)
        return (z, (x * SIDE + y) * 2 + core)

    opposite = ((z + 2) % N_DB, s)
    other_core = (z, block * 2 + 1 - core)
    along_v = [chip(u, (v + step) % SIDE) for step in (1, 3, 2)]
    along_u = [chip((u + step) % SIDE, v) for step in (1, 3, 2)]
    near = [((z + step) % N_DB, s) for step in (1, 3)]

    load_enc = pltpu.make_async_copy(encoded, enc, local_sem.at[0])
    load_q = pltpu.make_async_copy(queries, q, local_sem.at[1])
    load_wk = pltpu.make_async_copy(key_weight, wk, local_sem.at[2])
    load_wv = pltpu.make_async_copy(value_weight, wv, local_sem.at[3])
    load_enc.start()
    load_q.start()

    for g in range(2):
        for j in range(NB):
            wanted = shard[g, j] * BLK_SH + slot[g, j]
            mine[1 - g, j] = wanted
            if g == 0:
                req[z, 1, j] = wanted

    barrier = pltpu.get_barrier_semaphore()

    def tell(where):
        pl.semaphore_signal(barrier, inc=1, device_id=where, device_id_type=MESH)

    tell((z, ahead))
    for step in range(N_DB):
        tell(((z + step) % N_DB, behind))
    for partner in [*near, opposite, *along_v, *along_u, other_core]:
        tell(partner)
    pl.semaphore_wait(barrier, 15)

    brings = [None] * DIRECT
    row = sum(CHUNKS[:DIRECT])
    for c in range(DIRECT, n):
        rows = CHUNKS[c]
        half = rows // 2
        bring = pltpu.make_async_remote_copy(
            src_ref=encoded.at[block, pl.ds(row + core * half, half)], dst_ref=far[c].at[core, spot],
            send_sem=far_send.at[c, 0], recv_sem=far_recv.at[c, 0],
            device_id=opposite, device_id_type=MESH,
        )
        bring.start()
        brings.append(bring)
        row += rows

    asks = []
    for i, step in enumerate((0, 1, 3, 2)):
        for g in range(2):
            if g == 1 and step == 0:
                continue
            ask = pltpu.make_async_remote_copy(
                src_ref=mine.at[g], dst_ref=req.at[z, g],
                send_sem=req_send.at[g, i], recv_sem=req_recv.at[g, i],
                device_id=((z + step) % N_DB, ahead if g == 0 else s), device_id_type=MESH,
            )
            ask.start()
            asks.append(ask)
    give_q = pltpu.make_async_remote_copy(
        src_ref=queries.at[pl.ds(2 * CL - 16, 16)], dst_ref=q_prev,
        send_sem=q_sem.at[0], recv_sem=q_sem.at[1],
        device_id=(z, ahead), device_id_type=MESH,
    )
    give_q.start()

    def spread(c, first, pairs):
        moves = []
        for i, (partner, source) in enumerate(pairs):
            move = pltpu.make_async_remote_copy(
                src_ref=source, dst_ref=source,
                send_sem=far_send.at[c, first + i], recv_sem=far_recv.at[c, first + i],
                device_id=partner, device_id_type=MESH,
            )
            move.start()
            moves.append(move)
        return moves

    def wait_all(moves):
        for move in moves:
            move.wait()

    def pieces(c):
        brings[c].wait()
        return spread(c, 1, [(partner, far[c].at[core, spot]) for partner in along_v])

    def bundles(c, moves):
        wait_all(moves)
        held = far[c].at[core, pl.ds(u * SIDE, SIDE)]
        return spread(c, 4, [(partner, held) for partner in along_u])

    def share(c, moves):
        wait_all(moves)
        return spread(c, 7, [(other_core, far[c].at[core])])

    load_enc.wait()
    load_wk.start()
    load_wv.start()
    for ask in asks:
        ask.wait()

    def place_in(who, g, owner):
        first, second = req[who, g, 0], req[who, g, 1]
        from_second = jnp.where(second // BLK_SH == owner, second % BLK_SH, 0)
        return jnp.where(first // BLK_SH == owner, first % BLK_SH, from_second)

    places = [[place_in((z + step) % N_DB, g, z) for g in range(2)] for step in (0, 1, 3, 2)]
    far_places = [place_in(z, g, (z + 2) % N_DB) for g in range(2)]
    owners = [[req[z, g, j] // BLK_SH for j in range(NB)] for g in range(2)]
    blocks = []
    row = 0
    for c, rows in enumerate(CHUNKS):
        moves = []
        for i, partner in enumerate([*near, opposite] if c < DIRECT else near):
            for g in range(2):
                send[c][i, g] = enc[places[i + 1][g], row : row + rows, :]
            move = pltpu.make_async_remote_copy(
                src_ref=send[c].at[i], dst_ref=recv[c].at[z],
                send_sem=blk_send.at[c, i], recv_sem=blk_recv.at[c, i],
                device_id=partner, device_id_type=MESH,
            )
            move.start()
            moves.append(move)
        for g in range(2):
            recv[c][z, g] = enc[places[0][g], row : row + rows, :]
        blocks.append(moves)
        row += rows

    ones = [None] * DIRECT + [pieces(c) for c in range(DIRECT, n)]
    twos = [None] * DIRECT + [bundles(c, ones[c]) for c in range(DIRECT, n)]

    load_q.wait()
    give_q.wait()

    def shift_q(i, carry):
        cols = pl.ds(pl.multiple_of(i * 512, 512), 512)
        both = jnp.concatenate([q_prev[:, cols], q[:, cols]], axis=0).astype(jnp.float32)
        q_rows[:, cols] = pltpu.roll(both, 2 * CL + 1, 0)[: 2 * CL].astype(jnp.bfloat16)
        return carry

    lax.fori_loop(0, D // 512, shift_q, 0)

    shares = [[]] * n

    def advance(after):
        for c in PLAN.get(after, ()):
            shares[c] = share(c, twos[c])

    advance((-1, True))
    load_wk.wait()
    load_wv.wait()
    row = 0
    for c, rows in enumerate(CHUNKS):
        half = rows // 2
        for move in [*blocks[c], *shares[c]]:
            move.wait()
        for g in range(2 if c >= DIRECT else 0):
            at = far_places[g]
            recv[c][(z + 2) % N_DB, g, 0:half] = far[c][0, at]
            recv[c][(z + 2) % N_DB, g, half:rows] = far[c][1, at % SIDE * SIDE + at // SIDE]
        for g in range(2):
            for j in range(NB):
                at = (g * NB + j) * rows
                picks[at : at + rows, :] = recv[c][owners[g][j], g]
        for weight, held in ((wk, keys), (wv, values)):

            def project(i, carry, weight=weight, held=held, row=row, rows=rows):
                cols = pl.ds(pl.multiple_of(i * TILE, TILE), TILE)
                done = jnp.dot(
                    picks[0 : 4 * rows, :], weight[:, cols], preferred_element_type=jnp.float32
                ).astype(jnp.bfloat16)
                for g in range(2):
                    held[g, NB * row : NB * (row + rows), cols] = done[g * NB * rows : (g + 1) * NB * rows]
                return carry

            lax.fori_loop(0, D // TILE, project, 0)
            advance((c, weight is wv))
        row += rows

    def attend(g, half):
        heads = [pl.ds((half * HEADS + u) * HD, HD) for u in range(HEADS)]
        scores = [
            lax.dot_general(
                q_rows[g * CL : (g + 1) * CL, cols], keys[g, :, cols],
                (((1,), (1,)), ((), ())), preferred_element_type=jnp.float32,
            )
            for cols in heads
        ]
        tops = [jnp.max(score, axis=1, keepdims=True) for score in scores]
        raised = [jnp.exp2((score - top) * SCALE) for score, top in zip(scores, tops)]
        totals = [jnp.sum(each, axis=1, keepdims=True) for each in raised]
        weights = [
            (each * (1.0 / total)).astype(jnp.bfloat16) for each, total in zip(raised, totals)
        ]
        mixed = [
            jnp.dot(weight, values[g, :, cols], preferred_element_type=jnp.float32)
            for weight, cols in zip(weights, heads)
        ]
        return list(zip(heads, mixed))

    for half in range(H // HEADS):
        done = attend(0, half)
        for cols, each in done:
            moved = jnp.where(place == 0, 0.0, pltpu.roll(each, CL - 1, 0))
            out[0:CL, cols] = moved.astype(jnp.bfloat16)
        row_send[half * HEADS : (half + 1) * HEADS, :] = jnp.concatenate(
            [each[0:1] for _, each in done], axis=0
        ).astype(jnp.bfloat16)
    give_row = pltpu.make_async_remote_copy(
        src_ref=row_send, dst_ref=row_recv,
        send_sem=row_sem.at[0], recv_sem=row_sem.at[1],
        device_id=(z, behind), device_id_type=MESH,
    )
    give_row.start()
    for half in range(H // HEADS):
        for cols, each in attend(1, half):
            out[CL : 2 * CL, cols] = pltpu.roll(each, CL - 1, 0).astype(jnp.bfloat16)
            out[CL - 1 : CL, cols] = each[0:1].astype(jnp.bfloat16)
    give_row.wait()
    last = row_recv[...]
    for h in range(H):
        out[2 * CL - 1 : 2 * CL, h * HD : (h + 1) * HD] = last[h : h + 1]


def body(queries, encoded, key_weight, value_weight, nbr_shard, nbr_slot):
    n = len(CHUNKS)
    any_spec = pl.BlockSpec(memory_space=pl.ANY)
    smem = pl.BlockSpec(memory_space=pltpu.SMEM)
    bf16 = jnp.bfloat16
    return pl.pallas_call(
        kernel,
        out_shape=pltpu.VMEM((2 * CL, D), bf16),
        in_specs=[any_spec] * 4 + [smem] * 2,
        out_specs=pl.BlockSpec(memory_space=pltpu.VMEM),
        scratch_shapes=[
            pltpu.SMEM((2, NB), jnp.int32),
            pltpu.SMEM((N_DB, 2, NB), jnp.int32),
            pltpu.VMEM((BLK_SH, NT, DE), bf16),
            pltpu.VMEM((DE, D), bf16),
            pltpu.VMEM((DE, D), bf16),
            pltpu.VMEM((2 * CL, D), bf16),
            pltpu.VMEM((16, D), bf16),
            pltpu.VMEM((2 * CL, D), bf16),
            pltpu.VMEM((2, NB * NT, D), bf16),
            pltpu.VMEM((2, NB * NT, D), bf16),
            pltpu.VMEM((4 * max(CHUNKS), DE), bf16),
            pltpu.VMEM((H, HD), bf16),
            pltpu.VMEM((H, HD), bf16),
            *[pltpu.VMEM((3, 2, rows, DE), bf16) for rows in CHUNKS],
            *[pltpu.VMEM((N_DB, 2, rows, DE), bf16) for rows in CHUNKS],
            *[pltpu.VMEM((2, BLK_SH, rows // 2, DE), bf16) for rows in CHUNKS],
            pltpu.SemaphoreType.DMA((4,)),
            pltpu.SemaphoreType.DMA((2, N_DB)),
            pltpu.SemaphoreType.DMA((2, N_DB)),
            pltpu.SemaphoreType.DMA((n, 3)),
            pltpu.SemaphoreType.DMA((n, 3)),
            pltpu.SemaphoreType.DMA((n, 8)),
            pltpu.SemaphoreType.DMA((n, 8)),
            pltpu.SemaphoreType.DMA((2,)),
            pltpu.SemaphoreType.DMA((2,)),
        ],
        compiler_params=pltpu.CompilerParams(
            collective_id=0, has_side_effects=True, vmem_limit_bytes=58 << 20
        ),
        name="retro",
    )(queries, encoded, key_weight, value_weight, nbr_shard, nbr_slot)


def solution(mesh):
    placed = (
        P(("db", "seq"), None),
        P("db", None, None),
        P(),
        P(),
        P(("db", "seq"), None),
        P(("db", "seq"), None),
    )
    return jax.shard_map(
        body, mesh=mesh, in_specs=placed, out_specs=P(("db", "seq"), None), check_vma=False
    )
```

```python
import functools
import math

import jax
import jax.numpy as jnp
from jax import lax
from jax.experimental import pallas as pl
from jax.experimental.pallas import tpu as pltpu
from jax.sharding import PartitionSpec as P

H = 32
HD = 128
DE = 1024
D = 4096
CL = 64
NB = 2
NT = 128
LENGTH = 2048
BLK_SH = 16
N_DB = 4
SIDE = 4
PER_SEQ = 16
CHUNKS = (32, 32, 32, 32)
DIRECT = 1
PLAN = {(0, False): (1,), (1, False): (2,), (2, False): (3,)}
TILE = 4096
HEADS = 16
SCALE = math.log2(math.e) / math.sqrt(HD)
MESH = pl.DeviceIdType.MESH


def kernel(
    queries, encoded, key_weight, value_weight, shard, slot, out,
    mine, req, enc, wk, wv, q, q_prev, q_rows, keys, values, picks, row_send, row_recv,
    *rest,
):
    n = len(CHUNKS)
    send = rest[:n]
    recv = rest[n : 2 * n]
    far = rest[2 * n : 3 * n]
    (
        local_sem, req_send, req_recv, blk_send, blk_recv, far_send, far_recv, q_sem, row_sem,
    ) = rest[3 * n :]
    z = lax.axis_index("db")
    s = lax.axis_index("seq")
    base = (s // PER_SEQ) * PER_SEQ
    place = s % PER_SEQ
    ahead = base + (place + 1) % PER_SEQ
    behind = base + (place + PER_SEQ - 1) % PER_SEQ
    block, core = s // 2, s % 2
    u = jnp.where(core == 0, block // SIDE, block % SIDE)
    v = jnp.where(core == 0, block % SIDE, block // SIDE)
    spot = u * SIDE + v

    def chip(u_of, v_of):
        x = jnp.where(core == 0, u_of, v_of)
        y = jnp.where(core == 0, v_of, u_of)
        return (z, (x * SIDE + y) * 2 + core)

    opposite = ((z + 2) % N_DB, s)
    other_core = (z, block * 2 + 1 - core)
    along_v = [chip(u, (v + step) % SIDE) for step in (1, 3, 2)]
    along_u = [chip((u + step) % SIDE, v) for step in (1, 3, 2)]
    near = [((z + step) % N_DB, s) for step in (1, 3)]

    load_enc = pltpu.make_async_copy(encoded, enc, local_sem.at[0])
    load_q = pltpu.make_async_copy(queries, q, local_sem.at[1])
    load_wk = pltpu.make_async_copy(key_weight, wk, local_sem.at[2])
    load_wv = pltpu.make_async_copy(value_weight, wv, local_sem.at[3])
    load_enc.start()
    load_q.start()

    for g in range(2):
        for j in range(NB):
            wanted = shard[g, j] * BLK_SH + slot[g, j]
            mine[1 - g, j] = wanted
            if g == 0:
                req[z, 1, j] = wanted

    barrier = pltpu.get_barrier_semaphore()

    def tell(where):
        pl.semaphore_signal(barrier, inc=1, device_id=where, device_id_type=MESH)

    tell((z, ahead))
    for step in range(N_DB):
        tell(((z + step) % N_DB, behind))
    for partner in [*near, opposite, *along_v, *along_u, other_core]:
        tell(partner)
    pl.semaphore_wait(barrier, 15)

    brings = [None] * DIRECT
    row = sum(CHUNKS[:DIRECT])
    for c in range(DIRECT, n):
        rows = CHUNKS[c]
        half = rows // 2
        bring = pltpu.make_async_remote_copy(
            src_ref=encoded.at[block, pl.ds(row + core * half, half)], dst_ref=far[c].at[core, spot],
            send_sem=far_send.at[c, 0], recv_sem=far_recv.at[c, 0],
            device_id=opposite, device_id_type=MESH,
        )
        bring.start()
        brings.append(bring)
        row += rows

    asks = []
    for i, step in enumerate((0, 1, 3, 2)):
        for g in range(2):
            if g == 1 and step == 0:
                continue
            ask = pltpu.make_async_remote_copy(
                src_ref=mine.at[g], dst_ref=req.at[z, g],
                send_sem=req_send.at[g, i], recv_sem=req_recv.at[g, i],
                device_id=((z + step) % N_DB, ahead if g == 0 else s), device_id_type=MESH,
            )
            ask.start()
            asks.append(ask)
    give_q = pltpu.make_async_remote_copy(
        src_ref=queries.at[pl.ds(2 * CL - 16, 16)], dst_ref=q_prev,
        send_sem=q_sem.at[0], recv_sem=q_sem.at[1],
        device_id=(z, ahead), device_id_type=MESH,
    )
    give_q.start()

    def spread(c, first, pairs):
        moves = []
        for i, (partner, source) in enumerate(pairs):
            move = pltpu.make_async_remote_copy(
                src_ref=source, dst_ref=source,
                send_sem=far_send.at[c, first + i], recv_sem=far_recv.at[c, first + i],
                device_id=partner, device_id_type=MESH,
            )
            move.start()
            moves.append(move)
        return moves

    def wait_all(moves):
        for move in moves:
            move.wait()

    def pieces(c):
        brings[c].wait()
        return spread(c, 1, [(partner, far[c].at[core, spot]) for partner in along_v])

    def bundle(c, of):
        return far[c].at[core, pl.ds(of * SIDE, SIDE)]

    def bundles(c, moves):
        wait_all(moves)
        held = bundle(c, u)
        return spread(c, 4, [(partner, held) for partner in [*along_u, other_core]])

    def share(c, moves):
        shared = [moves[3]]
        for i, step in enumerate((3, 1, 2)):
            moves[i].wait()
            shared += spread(c, 8 + i, [(other_core, bundle(c, (u + step) % SIDE))])
        return shared

    ones = [None] * DIRECT + [pieces(DIRECT)]
    load_enc.wait()
    load_wk.start()
    load_wv.start()
    wait_all(asks[:5])

    def place_in(who, g, owner):
        first, second = req[who, g, 0], req[who, g, 1]
        from_second = jnp.where(second // BLK_SH == owner, second % BLK_SH, 0)
        return jnp.where(first // BLK_SH == owner, first % BLK_SH, from_second)

    def places(step):
        return [place_in((z + step) % N_DB, g, z) for g in range(2)]

    far_places = [place_in(z, g, (z + 2) % N_DB) for g in range(2)]
    owners = [[req[z, g, j] // BLK_SH for j in range(NB)] for g in range(2)]
    blocks = [[] for _ in CHUNKS]

    def direct(c, i, partner, at):
        row, rows = sum(CHUNKS[:c]), CHUNKS[c]
        for g in range(2):
            send[c][i, g] = enc[at[g], row : row + rows, :]
        move = pltpu.make_async_remote_copy(
            src_ref=send[c].at[i], dst_ref=recv[c].at[z],
            send_sem=blk_send.at[c, i], recv_sem=blk_recv.at[c, i],
            device_id=partner, device_id_type=MESH,
        )
        move.start()
        blocks[c].append(move)

    near_places = [places(1), places(3)]
    for c in range(DIRECT):
        for i, partner in enumerate(near):
            direct(c, i, partner, near_places[i])
    ones += [pieces(c) for c in range(DIRECT + 1, n)]
    wait_all(asks[5:])
    opposite_places = places(2)
    for c in range(DIRECT):
        direct(c, 2, opposite, opposite_places)
    for c in range(DIRECT, n):
        for i, partner in enumerate(near):
            direct(c, i, partner, near_places[i])
    twos = [None] * DIRECT + [bundles(c, ones[c]) for c in range(DIRECT, n)]
    own_places = places(0)
    row = 0
    for c, rows in enumerate(CHUNKS):
        for g in range(2):
            recv[c][z, g] = enc[own_places[g], row : row + rows, :]
        row += rows

    load_q.wait()
    give_q.wait()

    def shift_q(i, carry):
        cols = pl.ds(pl.multiple_of(i * 512, 512), 512)
        both = jnp.concatenate([q_prev[:, cols], q[:, cols]], axis=0).astype(jnp.float32)
        q_rows[:, cols] = pltpu.roll(both, 2 * CL + 1, 0)[: 2 * CL].astype(jnp.bfloat16)
        return carry

    lax.fori_loop(0, D // 512, shift_q, 0)

    shares = [[]] * n

    def advance(after):
        for c in PLAN.get(after, ()):
            shares[c] = share(c, twos[c])

    advance((-1, True))
    load_wk.wait()
    load_wv.wait()
    row = 0
    for c, rows in enumerate(CHUNKS):
        half = rows // 2
        for move in [*blocks[c], *shares[c]]:
            move.wait()
        for g in range(2 if c >= DIRECT else 0):
            at = far_places[g]
            recv[c][(z + 2) % N_DB, g, 0:half] = far[c][0, at]
            recv[c][(z + 2) % N_DB, g, half:rows] = far[c][1, at % SIDE * SIDE + at // SIDE]
        for g in range(2):
            for j in range(NB):
                at = (g * NB + j) * rows
                picks[at : at + rows, :] = recv[c][owners[g][j], g]
        for weight, held in ((wk, keys), (wv, values)):

            def project(i, carry, weight=weight, held=held, row=row, rows=rows):
                cols = pl.ds(pl.multiple_of(i * TILE, TILE), TILE)
                done = jnp.dot(
                    picks[0 : 4 * rows, :], weight[:, cols], preferred_element_type=jnp.float32
                ).astype(jnp.bfloat16)
                for g in range(2):
                    held[g, NB * row : NB * (row + rows), cols] = done[g * NB * rows : (g + 1) * NB * rows]
                return carry

            lax.fori_loop(0, D // TILE, project, 0)
            advance((c, weight is wv))
        row += rows

    def attend(g, half):
        heads = [pl.ds((half * HEADS + u) * HD, HD) for u in range(HEADS)]
        scores = [
            lax.dot_general(
                q_rows[g * CL : (g + 1) * CL, cols], keys[g, :, cols],
                (((1,), (1,)), ((), ())), preferred_element_type=jnp.float32,
            )
            for cols in heads
        ]
        tops = [jnp.max(score, axis=1, keepdims=True) for score in scores]
        raised = [jnp.exp2((score - top) * SCALE) for score, top in zip(scores, tops)]
        totals = [jnp.sum(each, axis=1, keepdims=True) for each in raised]
        weights = [
            (each * (1.0 / total)).astype(jnp.bfloat16) for each, total in zip(raised, totals)
        ]
        mixed = [
            jnp.dot(weight, values[g, :, cols], preferred_element_type=jnp.float32)
            for weight, cols in zip(weights, heads)
        ]
        return list(zip(heads, mixed))

    for half in range(H // HEADS):
        done = attend(0, half)
        for cols, each in done:
            moved = jnp.where(place == 0, 0.0, pltpu.roll(each, CL - 1, 0))
            out[0:CL, cols] = moved.astype(jnp.bfloat16)
        row_send[half * HEADS : (half + 1) * HEADS, :] = jnp.concatenate(
            [each[0:1] for _, each in done], axis=0
        ).astype(jnp.bfloat16)
    give_row = pltpu.make_async_remote_copy(
        src_ref=row_send, dst_ref=row_recv,
        send_sem=row_sem.at[0], recv_sem=row_sem.at[1],
        device_id=(z, behind), device_id_type=MESH,
    )
    give_row.start()
    for half in range(H // HEADS):
        for cols, each in attend(1, half):
            out[CL : 2 * CL, cols] = pltpu.roll(each, CL - 1, 0).astype(jnp.bfloat16)
            out[CL - 1 : CL, cols] = each[0:1].astype(jnp.bfloat16)
    give_row.wait()
    last = row_recv[...]
    for h in range(H):
        out[2 * CL - 1 : 2 * CL, h * HD : (h + 1) * HD] = last[h : h + 1]


def body(queries, encoded, key_weight, value_weight, nbr_shard, nbr_slot):
    n = len(CHUNKS)
    any_spec = pl.BlockSpec(memory_space=pl.ANY)
    smem = pl.BlockSpec(memory_space=pltpu.SMEM)
    bf16 = jnp.bfloat16
    return pl.pallas_call(
        kernel,
        out_shape=pltpu.VMEM((2 * CL, D), bf16),
        in_specs=[any_spec] * 4 + [smem] * 2,
        out_specs=pl.BlockSpec(memory_space=pltpu.VMEM),
        scratch_shapes=[
            pltpu.SMEM((2, NB), jnp.int32),
            pltpu.SMEM((N_DB, 2, NB), jnp.int32),
            pltpu.VMEM((BLK_SH, NT, DE), bf16),
            pltpu.VMEM((DE, D), bf16),
            pltpu.VMEM((DE, D), bf16),
            pltpu.VMEM((2 * CL, D), bf16),
            pltpu.VMEM((16, D), bf16),
            pltpu.VMEM((2 * CL, D), bf16),
            pltpu.VMEM((2, NB * NT, D), bf16),
            pltpu.VMEM((2, NB * NT, D), bf16),
            pltpu.VMEM((4 * max(CHUNKS), DE), bf16),
            pltpu.VMEM((H, HD), bf16),
            pltpu.VMEM((H, HD), bf16),
            *[pltpu.VMEM((3, 2, rows, DE), bf16) for rows in CHUNKS],
            *[pltpu.VMEM((N_DB, 2, rows, DE), bf16) for rows in CHUNKS],
            *[pltpu.VMEM((2, BLK_SH, rows // 2, DE), bf16) for rows in CHUNKS],
            pltpu.SemaphoreType.DMA((4,)),
            pltpu.SemaphoreType.DMA((2, N_DB)),
            pltpu.SemaphoreType.DMA((2, N_DB)),
            pltpu.SemaphoreType.DMA((n, 3)),
            pltpu.SemaphoreType.DMA((n, 3)),
            pltpu.SemaphoreType.DMA((n, 11)),
            pltpu.SemaphoreType.DMA((n, 11)),
            pltpu.SemaphoreType.DMA((2,)),
            pltpu.SemaphoreType.DMA((2,)),
        ],
        compiler_params=pltpu.CompilerParams(
            collective_id=0, has_side_effects=True, vmem_limit_bytes=58 << 20
        ),
        name="retro",
    )(queries, encoded, key_weight, value_weight, nbr_shard, nbr_slot)


def solution(mesh):
    placed = (
        P(("db", "seq"), None),
        P("db", None, None),
        P(),
        P(),
        P(("db", "seq"), None),
        P(("db", "seq"), None),
    )
    return jax.shard_map(
        body, mesh=mesh, in_specs=placed, out_specs=P(("db", "seq"), None), check_vma=False
    )
```

```python
import functools
import math

import jax
import jax.numpy as jnp
from jax import lax
from jax.experimental import pallas as pl
from jax.experimental.pallas import tpu as pltpu
from jax.sharding import PartitionSpec as P

H = 32
HD = 128
DE = 1024
D = 4096
CL = 64
NB = 2
NT = 128
LENGTH = 2048
BLK_SH = 16
N_DB = 4
SIDE = 4
PER_SEQ = 16
CHUNKS = (32, 32, 32, 32)
DIRECT = 1
PLAN = {(0, False): (1,), (1, False): (2,), (2, False): (3,)}
TILE = 4096
HEADS = 32
SCALE = math.log2(math.e) / math.sqrt(HD)
MESH = pl.DeviceIdType.MESH


def kernel(
    queries, encoded, key_weight, value_weight, shard, slot, out,
    mine, req, enc, wk, wv, q, q_prev, q_rows, keys, values, picks, row_send, row_recv,
    *rest,
):
    n = len(CHUNKS)
    send = rest[:n]
    recv = rest[n : 2 * n]
    far = rest[2 * n : 3 * n]
    (
        local_sem, req_send, req_recv, blk_send, blk_recv, far_send, far_recv, q_sem, row_sem,
    ) = rest[3 * n :]
    z = lax.axis_index("db")
    s = lax.axis_index("seq")
    base = (s // PER_SEQ) * PER_SEQ
    place = s % PER_SEQ
    ahead = base + (place + 1) % PER_SEQ
    behind = base + (place + PER_SEQ - 1) % PER_SEQ
    block, core = s // 2, s % 2
    u = jnp.where(core == 0, block // SIDE, block % SIDE)
    v = jnp.where(core == 0, block % SIDE, block // SIDE)
    spot = u * SIDE + v

    def chip(u_of, v_of):
        x = jnp.where(core == 0, u_of, v_of)
        y = jnp.where(core == 0, v_of, u_of)
        return (z, (x * SIDE + y) * 2 + core)

    opposite = ((z + 2) % N_DB, s)
    other_core = (z, block * 2 + 1 - core)
    along_v = [chip(u, (v + step) % SIDE) for step in (1, 3, 2)]
    along_u = [chip((u + step) % SIDE, v) for step in (1, 3, 2)]
    near = [((z + step) % N_DB, s) for step in (1, 3)]

    load_enc = pltpu.make_async_copy(encoded, enc, local_sem.at[0])
    load_q = pltpu.make_async_copy(queries, q, local_sem.at[1])
    load_wk = pltpu.make_async_copy(key_weight, wk, local_sem.at[2])
    load_wv = pltpu.make_async_copy(value_weight, wv, local_sem.at[3])
    load_enc.start()
    load_q.start()

    for g in range(2):
        for j in range(NB):
            wanted = shard[g, j] * BLK_SH + slot[g, j]
            mine[1 - g, j] = wanted
            if g == 0:
                req[z, 1, j] = wanted

    barrier = pltpu.get_barrier_semaphore()

    def tell(where):
        pl.semaphore_signal(barrier, inc=1, device_id=where, device_id_type=MESH)

    tell((z, ahead))
    for step in range(N_DB):
        tell(((z + step) % N_DB, behind))
    for partner in [*near, opposite, *along_v, *along_u, other_core]:
        tell(partner)
    pl.semaphore_wait(barrier, 15)

    brings = [None] * DIRECT
    row = sum(CHUNKS[:DIRECT])
    for c in range(DIRECT, n):
        rows = CHUNKS[c]
        half = rows // 2
        bring = pltpu.make_async_remote_copy(
            src_ref=encoded.at[block, pl.ds(row + core * half, half)], dst_ref=far[c].at[core, spot],
            send_sem=far_send.at[c, 0], recv_sem=far_recv.at[c, 0],
            device_id=opposite, device_id_type=MESH,
        )
        bring.start()
        brings.append(bring)
        row += rows

    asks = []
    for i, step in enumerate((0, 1, 3, 2)):
        for g in range(2):
            if g == 1 and step == 0:
                continue
            ask = pltpu.make_async_remote_copy(
                src_ref=mine.at[g], dst_ref=req.at[z, g],
                send_sem=req_send.at[g, i], recv_sem=req_recv.at[g, i],
                device_id=((z + step) % N_DB, ahead if g == 0 else s), device_id_type=MESH,
            )
            ask.start()
            asks.append(ask)
    give_q = pltpu.make_async_remote_copy(
        src_ref=queries.at[pl.ds(2 * CL - 16, 16)], dst_ref=q_prev,
        send_sem=q_sem.at[0], recv_sem=q_sem.at[1],
        device_id=(z, ahead), device_id_type=MESH,
    )
    give_q.start()

    def spread(c, first, pairs):
        moves = []
        for i, (partner, source) in enumerate(pairs):
            move = pltpu.make_async_remote_copy(
                src_ref=source, dst_ref=source,
                send_sem=far_send.at[c, first + i], recv_sem=far_recv.at[c, first + i],
                device_id=partner, device_id_type=MESH,
            )
            move.start()
            moves.append(move)
        return moves

    def wait_all(moves):
        for move in moves:
            move.wait()

    def pieces(c):
        brings[c].wait()
        return spread(c, 1, [(partner, far[c].at[core, spot]) for partner in along_v])

    def bundle(c, of):
        return far[c].at[core, pl.ds(of * SIDE, SIDE)]

    def bundles(c, moves):
        wait_all(moves)
        held = bundle(c, u)
        return spread(c, 4, [(partner, held) for partner in [*along_u, other_core]])

    def share(c, moves):
        shared = [moves[3]]
        for i, step in enumerate((3, 1, 2)):
            moves[i].wait()
            shared += spread(c, 8 + i, [(other_core, bundle(c, (u + step) % SIDE))])
        return shared

    ones = [None] * DIRECT + [pieces(DIRECT)]
    load_enc.wait()
    load_wk.start()
    load_wv.start()
    wait_all(asks[:5])

    def place_in(who, g, owner):
        first, second = req[who, g, 0], req[who, g, 1]
        from_second = jnp.where(second // BLK_SH == owner, second % BLK_SH, 0)
        return jnp.where(first // BLK_SH == owner, first % BLK_SH, from_second)

    def places(step):
        return [place_in((z + step) % N_DB, g, z) for g in range(2)]

    far_places = [place_in(z, g, (z + 2) % N_DB) for g in range(2)]
    owners = [[req[z, g, j] // BLK_SH for j in range(NB)] for g in range(2)]
    blocks = [[] for _ in CHUNKS]

    def direct(c, i, partner, at):
        row, rows = sum(CHUNKS[:c]), CHUNKS[c]
        for g in range(2):
            send[c][i, g] = enc[at[g], row : row + rows, :]
        move = pltpu.make_async_remote_copy(
            src_ref=send[c].at[i], dst_ref=recv[c].at[z],
            send_sem=blk_send.at[c, i], recv_sem=blk_recv.at[c, i],
            device_id=partner, device_id_type=MESH,
        )
        move.start()
        blocks[c].append(move)

    near_places = [places(1), places(3)]
    for c in range(DIRECT):
        for i, partner in enumerate(near):
            direct(c, i, partner, near_places[i])
    ones += [pieces(c) for c in range(DIRECT + 1, n)]
    wait_all(asks[5:])
    opposite_places = places(2)
    for c in range(DIRECT):
        direct(c, 2, opposite, opposite_places)
    for c in range(DIRECT, n):
        for i, partner in enumerate(near):
            direct(c, i, partner, near_places[i])
    twos = [None] * DIRECT + [bundles(c, ones[c]) for c in range(DIRECT, n)]
    own_places = places(0)
    row = 0
    for c, rows in enumerate(CHUNKS):
        for g in range(2):
            recv[c][z, g] = enc[own_places[g], row : row + rows, :]
        row += rows

    load_q.wait()
    give_q.wait()

    def shift_q(i, carry):
        cols = pl.ds(pl.multiple_of(i * 512, 512), 512)
        both = jnp.concatenate([q_prev[:, cols], q[:, cols]], axis=0).astype(jnp.float32)
        q_rows[:, cols] = pltpu.roll(both, 2 * CL + 1, 0)[: 2 * CL].astype(jnp.bfloat16)
        return carry

    lax.fori_loop(0, D // 512, shift_q, 0)

    shares = [[]] * n

    def advance(after):
        for c in PLAN.get(after, ()):
            shares[c] = share(c, twos[c])

    advance((-1, True))
    load_wk.wait()
    load_wv.wait()
    row = 0
    for c, rows in enumerate(CHUNKS):
        half = rows // 2
        for move in [*blocks[c], *shares[c]]:
            move.wait()
        for g in range(2 if c >= DIRECT else 0):
            at = far_places[g]
            recv[c][(z + 2) % N_DB, g, 0:half] = far[c][0, at]
            recv[c][(z + 2) % N_DB, g, half:rows] = far[c][1, at % SIDE * SIDE + at // SIDE]
        for g in range(2):
            for j in range(NB):
                at = (g * NB + j) * rows
                picks[at : at + rows, :] = recv[c][owners[g][j], g]
        for weight, held in ((wk, keys), (wv, values)):

            def project(i, carry, weight=weight, held=held, row=row, rows=rows):
                cols = pl.ds(pl.multiple_of(i * TILE, TILE), TILE)
                done = jnp.dot(
                    picks[0 : 4 * rows, :], weight[:, cols], preferred_element_type=jnp.float32
                ).astype(jnp.bfloat16)
                for g in range(2):
                    held[g, NB * row : NB * (row + rows), cols] = done[g * NB * rows : (g + 1) * NB * rows]
                return carry

            lax.fori_loop(0, D // TILE, project, 0)
            advance((c, weight is wv))
        row += rows

    def attend(g, half):
        heads = [pl.ds((half * HEADS + u) * HD, HD) for u in range(HEADS)]
        scores = [
            lax.dot_general(
                q_rows[g * CL : (g + 1) * CL, cols], keys[g, :, cols],
                (((1,), (1,)), ((), ())), preferred_element_type=jnp.float32,
            )
            for cols in heads
        ]
        tops = [jnp.max(score, axis=1, keepdims=True) for score in scores]
        raised = [jnp.exp2((score - top) * SCALE) for score, top in zip(scores, tops)]
        totals = [jnp.sum(each, axis=1, keepdims=True) for each in raised]
        weights = [
            (each * (1.0 / total)).astype(jnp.bfloat16) for each, total in zip(raised, totals)
        ]
        mixed = [
            jnp.dot(weight, values[g, :, cols], preferred_element_type=jnp.float32)
            for weight, cols in zip(weights, heads)
        ]
        return list(zip(heads, mixed))

    for half in range(H // HEADS):
        done = attend(0, half)
        for cols, each in done:
            moved = jnp.where(place == 0, 0.0, pltpu.roll(each, CL - 1, 0))
            out[0:CL, cols] = moved.astype(jnp.bfloat16)
        row_send[half * HEADS : (half + 1) * HEADS, :] = jnp.concatenate(
            [each[0:1] for _, each in done], axis=0
        ).astype(jnp.bfloat16)
    give_row = pltpu.make_async_remote_copy(
        src_ref=row_send, dst_ref=row_recv,
        send_sem=row_sem.at[0], recv_sem=row_sem.at[1],
        device_id=(z, behind), device_id_type=MESH,
    )
    give_row.start()
    for half in range(H // HEADS):
        for cols, each in attend(1, half):
            out[CL : 2 * CL, cols] = pltpu.roll(each, CL - 1, 0).astype(jnp.bfloat16)
            out[CL - 1 : CL, cols] = each[0:1].astype(jnp.bfloat16)
    give_row.wait()
    last = row_recv[...]
    for h in range(H):
        out[2 * CL - 1 : 2 * CL, h * HD : (h + 1) * HD] = last[h : h + 1]


def body(queries, encoded, key_weight, value_weight, nbr_shard, nbr_slot):
    n = len(CHUNKS)
    any_spec = pl.BlockSpec(memory_space=pl.ANY)
    smem = pl.BlockSpec(memory_space=pltpu.SMEM)
    bf16 = jnp.bfloat16
    return pl.pallas_call(
        kernel,
        out_shape=pltpu.VMEM((2 * CL, D), bf16),
        in_specs=[any_spec] * 4 + [smem] * 2,
        out_specs=pl.BlockSpec(memory_space=pltpu.VMEM),
        scratch_shapes=[
            pltpu.SMEM((2, NB), jnp.int32),
            pltpu.SMEM((N_DB, 2, NB), jnp.int32),
            pltpu.VMEM((BLK_SH, NT, DE), bf16),
            pltpu.VMEM((DE, D), bf16),
            pltpu.VMEM((DE, D), bf16),
            pltpu.VMEM((2 * CL, D), bf16),
            pltpu.VMEM((16, D), bf16),
            pltpu.VMEM((2 * CL, D), bf16),
            pltpu.VMEM((2, NB * NT, D), bf16),
            pltpu.VMEM((2, NB * NT, D), bf16),
            pltpu.VMEM((4 * max(CHUNKS), DE), bf16),
            pltpu.VMEM((H, HD), bf16),
            pltpu.VMEM((H, HD), bf16),
            *[pltpu.VMEM((3, 2, rows, DE), bf16) for rows in CHUNKS],
            *[pltpu.VMEM((N_DB, 2, rows, DE), bf16) for rows in CHUNKS],
            *[pltpu.VMEM((2, BLK_SH, rows // 2, DE), bf16) for rows in CHUNKS],
            pltpu.SemaphoreType.DMA((4,)),
            pltpu.SemaphoreType.DMA((2, N_DB)),
            pltpu.SemaphoreType.DMA((2, N_DB)),
            pltpu.SemaphoreType.DMA((n, 3)),
            pltpu.SemaphoreType.DMA((n, 3)),
            pltpu.SemaphoreType.DMA((n, 11)),
            pltpu.SemaphoreType.DMA((n, 11)),
            pltpu.SemaphoreType.DMA((2,)),
            pltpu.SemaphoreType.DMA((2,)),
        ],
        compiler_params=pltpu.CompilerParams(
            collective_id=0, has_side_effects=True, vmem_limit_bytes=58 << 20
        ),
        name="retro",
    )(queries, encoded, key_weight, value_weight, nbr_shard, nbr_slot)


def solution(mesh):
    placed = (
        P(("db", "seq"), None),
        P("db", None, None),
        P(),
        P(),
        P(("db", "seq"), None),
        P(("db", "seq"), None),
    )
    return jax.shard_map(
        body, mesh=mesh, in_specs=placed, out_specs=P(("db", "seq"), None), check_vma=False
    )
```
